32 devices in a mesh: parts: 2 (over y), blk: 16 (over z, x, core).
Axes of the slice: x: 2, y: 2, z: 4, core: 2. Of those that a mesh axis runs over, the one named last changes fastest.
Arguments:
- student: bfloat16 [6144, 3584], P(('parts', 'blk')), parts along dimension 0, may hold values from -6 to 6, as said below
- teacher: bfloat16 [6144, 3584], P(('parts', 'blk')), parts along dimension 0, may hold values from -6 to 6, as said below
Outputs:
- grad: bfloat16 [6144, 3584], P(('parts', 'blk')), parts along dimension 0
- row_loss: float32 [6144], P(('parts', 'blk')), parts along dimension 0
The draws below stay inside these ranges and needn't reach their ends.
There are 2 independent parts, one for each index of `parts`. The reference program is written for one: setup_inputs(seed, part) draws one part's arguments, and reference() takes and returns one part's arrays. A program takes and returns all parts, laid end to end along the dimension named above; each array names one. Nothing has to cross between parts.
Inputs may be any that keep to these rules, and one draw needn't show every extreme that they name: `student`: hidden states of one token per row. `teacher`: hidden states of one token per row.
All inputs are finite; a program needn't handle non-finite values.
Results may differ from the reference program's by a relative error of at most 0.0047.
Values may be sent and summed in bfloat16 or wider, within the bound.
No kernel may reach another device: no remote copies, remote signals or barrier semaphores. Data moves between devices by JAX's collectives and lax.ppermute only.
A program may use at most 64 MiB of HBM per device.

```python
import math
import jax
import jax.numpy as jnp
from jax import lax

D = 3584
TOK_DEV = 192
REACH = 4
TOKENS = 3072
WINDOW = 1728
N_BLK = 16


def shared_rows(key, lower, upper):
    scale_key, normal_key = jax.random.split(key, 2)
    row_scale = jnp.exp(jax.random.uniform(scale_key, (TOKENS, 1), jnp.float32, math.log(lower), math.log(upper)))
    normal_part = jax.random.normal(normal_key, (TOKENS, D), jnp.float32)
    return (row_scale, normal_part)


def draw_student(key, part):
    row_scale, base = shared_rows(key, 0.5, 1.6)
    values = row_scale * base
    return jnp.clip(values, -6.0, 6.0).astype(jnp.bfloat16)


def draw_teacher(key, part):
    row_scale, base = shared_rows(key, 0.5, 1.6)
    key = jax.random.fold_in(key, 7)
    noise = jax.random.normal(key, (TOKENS, D), jnp.float32)
    values = row_scale * (0.6 * base + 0.8 * noise)
    return jnp.clip(values, -6.0, 6.0).astype(jnp.bfloat16)


def setup_inputs(seed: int = 0, part: int = 0) -> dict:
    keys = jax.random.split(jax.random.key(seed), 3)
    part_keys = jax.random.split(jax.random.fold_in(keys[2], part), 3)
    student = draw_student(jax.random.fold_in(jax.random.fold_in(keys[2], part), 71), part)
    teacher = draw_teacher(jax.random.fold_in(jax.random.fold_in(keys[2], part), 71), part)
    return dict(student=student, teacher=teacher)


def reference(student, teacher):
    scale = 1.0 / math.sqrt(D)
    margin = REACH * TOK_DEV
    padded_student = jnp.pad(student, ((margin, margin), (0, 0)))
    padded_teacher = jnp.pad(teacher, ((margin, margin), (0, 0)))

    def one_block(index):
        start = (index * TOK_DEV).astype(jnp.int32)
        own_student = lax.dynamic_slice_in_dim(student, start, TOK_DEV, 0)
        own_teacher = lax.dynamic_slice_in_dim(teacher, start, TOK_DEV, 0)
        band_student = lax.dynamic_slice_in_dim(padded_student, start, WINDOW, 0)
        band_teacher = lax.dynamic_slice_in_dim(padded_teacher, start, WINDOW, 0)
        student_gram = jnp.dot(own_student, band_student.T, preferred_element_type=jnp.float32)
        teacher_gram = jnp.dot(own_teacher, band_teacher.T, preferred_element_type=jnp.float32)
        gap = (student_gram - teacher_gram) * scale
        rows = lax.optimization_barrier(jnp.sum(gap * gap, axis=1)) / WINDOW
        gap_b = gap.astype(jnp.bfloat16)
        block_grad = jnp.dot(gap_b, band_student, preferred_element_type=jnp.float32) / math.sqrt(WINDOW)
        return (block_grad.astype(jnp.bfloat16), rows)
    grads, rows = lax.map(one_block, jnp.arange(N_BLK, dtype=jnp.int32))
    return (grads.reshape(TOKENS, D), rows.reshape(TOKENS))
```

```python
import math

import jax
import jax.numpy as jnp
from jax import lax
from jax.sharding import PartitionSpec as P

REACH = 4
AXIS = "blk"


def move(block, target):
    devices = range(lax.axis_size(AXIS))
    route = [(i, target(i)) for i in devices if target(i) is not None and target(i) in devices]
    return lax.ppermute(block, AXIS, route)


def odd_chip(i):
    return (i // 2) % 2


def partner(i):
    return i ^ 2


def heavy(i):
    return i + 4 if odd_chip(i) else i - 4


def light(i):
    return i - 4 if odd_chip(i) else i + 4


def swap(i):
    return i ^ 1


def outer(i):
    return (i % 2) ^ odd_chip(i)


def swap_to_outer(i):
    return None if outer(i) else i ^ 1


def swap_to_inner(i):
    return i ^ 1 if outer(i) else None


def gram(a, b):
    return lax.dot_general(a, b, (((1,), (1,)), ((), ())), preferred_element_type=jnp.float32)


def body(student, teacher):
    rows, width = student.shape
    window = (2 * REACH + 1) * rows
    scale = 1.0 / math.sqrt(width)
    index = lax.axis_index(AXIS)
    inner = (1 - ((index % 2) ^ ((index // 2) % 2))).astype(jnp.float32)

    def gap(s, t, other_s, other_t, factor=scale):
        return (gram(s, other_s) - gram(t, other_t)) * factor

    t_far = move(teacher, heavy)
    s_side = move(student, partner)
    s_back = move(student, light)
    s_mate = move(student, swap)
    t_mate = move(teacher, swap)
    s_far = move(student, heavy)
    t_side = move(teacher, partner)
    s_diag = move(s_side, light)
    s_side_mate = move(s_side, swap)
    s_back_mate = move(s_back, swap_to_inner)
    t_far_mate = move(t_far, swap_to_outer)
    s_far_mate = move(s_far, swap_to_outer)
    t_side_mate = move(t_side, swap)
    s_diag_mate = move(s_diag, swap)

    out_gap = jnp.concatenate(
        [
            gap(s_far, t_far, student, teacher),
            gap(s_far, t_far, s_mate, t_mate, scale * inner),
            gap(s_far, t_far, s_side, t_side),
            gap(s_far, t_far, s_side_mate, t_side_mate),
        ],
        axis=1,
    ).astype(jnp.bfloat16)
    in_gap = move(out_gap, light)

    pairs = [
        (student, teacher),
        (s_mate, t_mate),
        (s_side, t_side),
        (s_side_mate, t_side_mate),
        (s_far, t_far),
        (s_far_mate, t_far_mate),
    ]
    grad = jnp.zeros((rows, width), jnp.float32)
    row_sum = jnp.zeros((rows,), jnp.float32)
    for other_s, other_t in pairs:
        g = gap(student, teacher, other_s, other_t)
        row_sum = row_sum + jnp.sum(g * g, axis=1)
        grad = grad + jnp.dot(g.astype(jnp.bfloat16), other_s, preferred_element_type=jnp.float32)
    wide = in_gap.astype(jnp.float32)
    row_sum = row_sum + jnp.sum(wide * wide, axis=1)
    for k, other_s in enumerate((s_back, s_back_mate, s_diag, s_diag_mate)):
        g = in_gap[:, k * rows : (k + 1) * rows]
        grad = grad + jnp.dot(g, other_s, preferred_element_type=jnp.float32)
    return ((grad / math.sqrt(window)).astype(jnp.bfloat16), row_sum / window)


def solution(mesh):
    return jax.shard_map(
        body,
        mesh=mesh,
        in_specs=(P(("parts", "blk"), None), P(("parts", "blk"), None)),
        out_specs=(P(("parts", "blk"), None), P(("parts", "blk"))),
        check_vma=False,
    )
```

```python
import functools
import math

import jax
import jax.numpy as jnp
from jax import lax
from jax.experimental import pallas as pl
from jax.experimental.pallas import tpu as pltpu
from jax.sharding import PartitionSpec as P

REACH = 4
AXIS = "blk"
LANES = 128
VMEM_BYTES = 9 * 1024 * 1024


def move(block, target):
    devices = range(lax.axis_size(AXIS))
    route = [(i, target(i)) for i in devices if target(i) is not None and target(i) in devices]
    return lax.ppermute(block, AXIS, route)


def odd_chip(i):
    return (i // 2) % 2


def partner(i):
    return i ^ 2


def heavy(i):
    return i + 4 if odd_chip(i) else i - 4


def light(i):
    return i - 4 if odd_chip(i) else i + 4


def swap(i):
    return i ^ 1


def outer(i):
    return (i % 2) ^ odd_chip(i)


def swap_to_outer(i):
    return None if outer(i) else i ^ 1


def swap_to_inner(i):
    return i ^ 1 if outer(i) else None


def after(block, *others):
    return lax.optimization_barrier((block, *others))[0]


def gram(a, b):
    return lax.dot_general(a, b, (((1,), (1,)), ((), ())), preferred_element_type=jnp.float32)


def lane_sums(x):
    total = x[:, :LANES]
    for k in range(1, x.shape[1] // LANES):
        total = total + x[:, k * LANES : (k + 1) * LANES]
    return total


def columns(width):
    for tile in (512, 384, 256, 128):
        if width % tile == 0:
            return tile
    return width


def call(kernel, ins, outs, scratch, flops, name):
    nbytes = sum(x.size * x.dtype.itemsize for x in ins) + sum(math.prod(o.shape) * o.dtype.itemsize for o in outs)
    spec = pl.BlockSpec(memory_space=pltpu.VMEM)
    return pl.pallas_call(
        kernel,
        in_specs=[spec] * len(ins),
        out_specs=[spec] * len(outs),
        out_shape=outs,
        scratch_shapes=scratch,
        cost_estimate=pl.CostEstimate(flops=int(flops), bytes_accessed=int(nbytes), transcendentals=0),
        compiler_params=pltpu.CompilerParams(vmem_limit_bytes=VMEM_BYTES),
        name=name,
    )(*ins)


def grams(rows_of, others, store):
    rows = rows_of.shape[0]
    for j, other in enumerate(others):
        store(slice(j * rows, (j + 1) * rows), gram(rows_of[...], other[...]))


def weigh(gap_b, others, put):
    width = others[0].shape[1]
    tile = columns(width)
    for k in range(width // tile):
        at = slice(k * tile, (k + 1) * tile)
        stack = jnp.concatenate([other[:, at] for other in others], axis=0)
        put(at, jnp.dot(gap_b[...], stack, preferred_element_type=jnp.float32))


def own_kernel(scale, s, t, s_mate, t_mate, grad, sums, gap_b):
    rows = s.shape[0]
    for j, (os, ot) in enumerate(((s, t), (s_mate, t_mate))):
        g = (gram(s[...], os[...]) - gram(t[...], ot[...])) * scale
        gap_b[:, j * rows : (j + 1) * rows] = g.astype(jnp.bfloat16)
    wide = gap_b[...].astype(jnp.float32)
    sums[...] = lane_sums(wide * wide)

    def put(at, value):
        grad[:, at] = value

    weigh(gap_b, (s, s_mate), put)


def own_part(s, t, s_mate, t_mate, scale):
    rows, width = s.shape
    return call(
        functools.partial(own_kernel, scale),
        (s, t, s_mate, t_mate),
        [jax.ShapeDtypeStruct((rows, width), jnp.float32), jax.ShapeDtypeStruct((rows, LANES), jnp.float32)],
        [pltpu.VMEM((rows, 2 * rows), jnp.bfloat16)],
        512 * rows * rows * width,
        "own_part",
    )


def student_grams_kernel(s, s_mate, x, x_mate, f, f_mate, mine, out):
    def store_mine(at, value):
        mine[:, at] = value

    def store_out(at, value):
        out[:, at] = value

    grams(s, (x, x_mate, f, f_mate), store_mine)
    grams(f, (s, s_mate, x, x_mate), store_out)


def student_grams(*blocks):
    rows, width = blocks[0].shape
    shape = jax.ShapeDtypeStruct((rows, 4 * rows), jnp.float32)
    return call(student_grams_kernel, blocks, [shape, shape], [], 16 * rows * rows * width, "student_grams")


def send_gap_kernel(f, t, t_mate, x, x_mate, student, factors, out):
    def store(at, value):
        out[:, at] = ((student[:, at] - value) * factors[:, at]).astype(jnp.bfloat16)

    grams(f, (t, t_mate, x, x_mate), store)


def send_gap(f, t, t_mate, x, x_mate, student, factors):
    rows, width = f.shape
    return call(
        send_gap_kernel,
        (f, t, t_mate, x, x_mate, student, factors),
        [jax.ShapeDtypeStruct((rows, 4 * rows), jnp.bfloat16)],
        [],
        512 * rows * rows * width,
        "send_gap",
    )[0]


def near_kernel(scale, t, tx, tx_mate, tf, tf_mate, student, sx, sx_mate, sf, sf_mate, grad_in, sums_in, grad, sums, gap_b):
    def store(at, value):
        gap_b[:, at] = ((student[:, at] - value) * scale).astype(jnp.bfloat16)

    grams(t, (tx, tx_mate, tf, tf_mate), store)
    wide = gap_b[...].astype(jnp.float32)
    sums[...] = sums_in[...] + lane_sums(wide * wide)

    def put(at, value):
        grad[:, at] = grad_in[:, at] + value

    weigh(gap_b, (sx, sx_mate, sf, sf_mate), put)


def near_part(t, tx, tx_mate, tf, tf_mate, student, sx, sx_mate, sf, sf_mate, grad_in, sums_in, scale):
    rows, width = t.shape
    return call(
        functools.partial(near_kernel, scale),
        (t, tx, tx_mate, tf, tf_mate, student, sx, sx_mate, sf, sf_mate, grad_in, sums_in),
        [jax.ShapeDtypeStruct((rows, width), jnp.float32), jax.ShapeDtypeStruct((rows, LANES), jnp.float32)],
        [pltpu.VMEM((rows, 4 * rows), jnp.bfloat16)],
        16 * rows * rows * width,
        "near_part",
    )


def last_kernel(scale, gap_b, a, b, c, d, grad_in, sums_in, grad, sums):
    def put(at, value):
        grad[:, at] = ((grad_in[:, at] + value) * scale).astype(grad.dtype)

    weigh(gap_b, (a, b, c, d), put)
    wide = gap_b[...].astype(jnp.float32)
    sums[...] = sums_in[...] + lane_sums(wide * wide)


def last_part(gap_b, a, b, c, d, grad_in, sums_in, scale):
    rows, width = a.shape
    return call(
        functools.partial(last_kernel, scale),
        (gap_b, a, b, c, d, grad_in, sums_in),
        [jax.ShapeDtypeStruct((rows, width), jnp.bfloat16), jax.ShapeDtypeStruct((rows, LANES), jnp.float32)],
        [],
        8 * rows * rows * width,
        "last_part",
    )


def body(student, teacher):
    rows, width = student.shape
    window = (2 * REACH + 1) * rows
    scale = 1.0 / math.sqrt(width)
    index = lax.axis_index(AXIS)
    inner = (1 - ((index % 2) ^ ((index // 2) % 2))).astype(jnp.float32)
    lane = lax.broadcasted_iota(jnp.int32, (1, 4 * rows), 1)
    factors = jnp.where((lane >= rows) & (lane < 2 * rows), scale * inner, scale)

    s_side = move(student, partner)
    s_far = move(student, heavy)
    s_back = move(student, light)
    s_mate = move(student, swap)
    t_mate = move(teacher, swap)
    t_side = move(after(teacher, s_side), partner)
    t_far = move(after(teacher, s_far), heavy)
    s_diag = move(after(s_side, s_back), light)

    grad, sums = own_part(student, teacher, s_mate, t_mate, scale)
    s_side_mate = move(s_side, swap)
    s_far_mate = move(s_far, swap_to_outer)
    s_back_mate = move(after(s_back, s_side_mate, s_far_mate), swap_to_inner)
    mine, out = student_grams(student, s_mate, s_side, s_side_mate, s_far, s_far_mate)

    t_side_mate = move(after(t_side, out), swap)
    t_far_mate = move(after(t_far, out), swap_to_outer)
    s_diag_mate = move(s_diag, swap)
    out_gap = send_gap(t_far, teacher, t_mate, t_side, t_side_mate, out, factors)
    in_gap = move(out_gap, light)
    grad, sums = near_part(
        teacher, t_side, t_side_mate, t_far, t_far_mate, mine,
        s_side, s_side_mate, s_far, s_far_mate, grad, sums, scale,
    )
    grad, sums = last_part(in_gap, s_back, s_back_mate, s_diag, s_diag_mate, grad, sums, 1.0 / math.sqrt(window))
    return grad, jnp.sum(sums, axis=1) / window


def solution(mesh):
    return jax.shard_map(
        body,
        mesh=mesh,
        in_specs=(P(("parts", "blk"), None), P(("parts", "blk"), None)),
        out_specs=(P(("parts", "blk"), None), P(("parts", "blk"))),
        check_vma=False,
    )
```

```python
import functools
import math

import jax
import jax.numpy as jnp
from jax import lax
from jax.experimental import pallas as pl
from jax.experimental.pallas import tpu as pltpu
from jax.sharding import PartitionSpec as P

REACH = 4
AXIS = "blk"
LANES = 128
VMEM_BYTES = 9 * 1024 * 1024


def move(block, target):
    devices = range(lax.axis_size(AXIS))
    route = [(i, target(i)) for i in devices if target(i) is not None and target(i) in devices]
    return lax.ppermute(block, AXIS, route)


def odd_chip(i):
    return (i // 2) % 2


def partner(i):
    return i ^ 2


def heavy(i):
    return i + 4 if odd_chip(i) else i - 4


def light(i):
    return i - 4 if odd_chip(i) else i + 4


def swap(i):
    return i ^ 1


def after(block, *others):
    return lax.optimization_barrier((block, *others))[0]


def gram(a, b):
    return lax.dot_general(a, b, (((1,), (1,)), ((), ())), preferred_element_type=jnp.float32)


def lane_sums(x):
    total = x[:, :LANES]
    for k in range(1, x.shape[1] // LANES):
        total = total + x[:, k * LANES : (k + 1) * LANES]
    return total


def columns(width):
    for tile in (512, 384, 256, 128):
        if width % tile == 0:
            return tile
    return width


def call(kernel, ins, outs, scratch, flops, name, alias=None):
    nbytes = sum(x.size * x.dtype.itemsize for x in ins) + sum(math.prod(o.shape) * o.dtype.itemsize for o in outs)
    spec = pl.BlockSpec(memory_space=pltpu.VMEM)
    return pl.pallas_call(
        kernel,
        in_specs=[spec] * len(ins),
        out_specs=[spec] * len(outs),
        out_shape=outs,
        scratch_shapes=scratch,
        cost_estimate=pl.CostEstimate(flops=int(flops), bytes_accessed=int(nbytes), transcendentals=0),
        compiler_params=pltpu.CompilerParams(vmem_limit_bytes=VMEM_BYTES),
        input_output_aliases=alias or {},
        name=name,
    )(*ins)


def grams(rows_of, others, store):
    rows = rows_of.shape[0]
    for j, other in enumerate(others):
        store(slice(j * rows, (j + 1) * rows), gram(rows_of[...], other[...]))


def weigh(gap_b, others, put):
    width = others[0].shape[1]
    tile = columns(width)
    for k in range(width // tile):
        at = slice(k * tile, (k + 1) * tile)
        stack = jnp.concatenate([other[:, at] for other in others], axis=0)
        put(at, jnp.dot(gap_b[...], stack, preferred_element_type=jnp.float32))


def own_kernel(scale, s, t, s_mate, t_mate, grad, sums, gap_b):
    rows = s.shape[0]
    for j, (os, ot) in enumerate(((s, t), (s_mate, t_mate))):
        g = (gram(s[...], os[...]) - gram(t[...], ot[...])) * scale
        gap_b[:, j * rows : (j + 1) * rows] = g.astype(jnp.bfloat16)
    wide = gap_b[...].astype(jnp.float32)
    sums[...] = lane_sums(wide * wide)

    def put(at, value):
        grad[:, at] = value

    weigh(gap_b, (s, s_mate), put)


def own_part(s, t, s_mate, t_mate, scale):
    rows, width = s.shape
    return call(
        functools.partial(own_kernel, scale),
        (s, t, s_mate, t_mate),
        [jax.ShapeDtypeStruct((rows, width), jnp.float32), jax.ShapeDtypeStruct((rows, LANES), jnp.float32)],
        [pltpu.VMEM((rows, 2 * rows), jnp.bfloat16)],
        12 * rows * rows * width,
        "own_part",
    )


def student_grams_kernel(s, s_mate, x, x_mate, f, mine, out):
    def store_mine(at, value):
        mine[:, at] = value

    def store_out(at, value):
        out[:, at] = value

    grams(s, (x, x_mate, f), store_mine)
    grams(f, (s, s_mate, x, x_mate), store_out)


def student_grams(*blocks):
    rows, width = blocks[0].shape
    shapes = [jax.ShapeDtypeStruct((rows, n * rows), jnp.float32) for n in (3, 4)]
    return call(student_grams_kernel, blocks, shapes, [], 14 * rows * rows * width, "student_grams")


def send_direct_kernel(f, t, t_mate, student, factors, out, cross):
    def store(at, value):
        g = ((student[:, at] - value) * factors[:, at]).astype(jnp.bfloat16)
        out[:, at] = g
        if at.start:
            cross[...] = g

    grams(f, (t, t_mate), store)


def send_direct(f, t, t_mate, student, factors):
    rows, width = f.shape
    return call(
        send_direct_kernel,
        (f, t, t_mate, student, factors),
        [jax.ShapeDtypeStruct((rows, 4 * rows), jnp.bfloat16), jax.ShapeDtypeStruct((rows, rows), jnp.bfloat16)],
        [],
        4 * rows * rows * width,
        "send_direct",
    )


def send_diag_kernel(scale, f, x, x_mate, student, direct, out):
    rows = f.shape[0]
    out[:, : 2 * rows] = direct[:, : 2 * rows]
    for j, other in enumerate((x, x_mate)):
        at = slice((j + 2) * rows, (j + 3) * rows)
        out[:, at] = ((student[:, at] - gram(f[...], other[...])) * scale).astype(jnp.bfloat16)


def send_diag(f, x, x_mate, student, direct, scale):
    rows, width = f.shape
    return call(
        functools.partial(send_diag_kernel, scale),
        (f, x, x_mate, student, direct),
        [jax.ShapeDtypeStruct((rows, 4 * rows), jnp.bfloat16)],
        [],
        4 * rows * rows * width,
        "send_diag",
    )[0]


def near_kernel(scale, t, tx, tx_mate, tf, student, cross, sx, sx_mate, sf, sf_mate, grad_in, sums_in, grad, sums, gap_b):
    rows = t.shape[0]

    def store(at, value):
        gap_b[:, at] = ((student[:, at] - value) * scale).astype(jnp.bfloat16)

    grams(t, (tx, tx_mate, tf), store)
    gap_b[:, 3 * rows :] = cross[...].astype(jnp.float32).T.astype(jnp.bfloat16)
    wide = gap_b[...].astype(jnp.float32)
    sums[...] = sums_in[...] + lane_sums(wide * wide)

    def put(at, value):
        grad[:, at] = grad_in[:, at] + value

    weigh(gap_b, (sx, sx_mate, sf, sf_mate), put)


def near_part(t, tx, tx_mate, tf, student, cross, sx, sx_mate, sf, sf_mate, grad_in, sums_in, scale):
    rows, width = t.shape
    return call(
        functools.partial(near_kernel, scale),
        (t, tx, tx_mate, tf, student, cross, sx, sx_mate, sf, sf_mate, grad_in, sums_in),
        [jax.ShapeDtypeStruct((rows, width), jnp.float32), jax.ShapeDtypeStruct((rows, LANES), jnp.float32)],
        [pltpu.VMEM((rows, 4 * rows), jnp.bfloat16)],
        14 * rows * rows * width,
        "near_part",
        {10: 0, 11: 1},
    )


def last_kernel(scale, weight, gap_b, a, b, c, d, grad_in, sums_in, grad, sums, held, sems):
    width = a.shape[1]
    tile = columns(width)
    copies = []
    wide = gap_b[...].astype(jnp.float32)
    total = sums_in[...] + lane_sums(wide * wide)
    sums[...] = jnp.sum(total.T, axis=0, keepdims=True) * weight
    for k in range(width // tile):
        at = slice(k * tile, (k + 1) * tile)
        stack = jnp.concatenate([other[:, at] for other in (a, b, c, d)], axis=0)
        value = jnp.dot(gap_b[...], stack, preferred_element_type=jnp.float32)
        held[:, at] = ((grad_in[:, at] + value) * scale).astype(grad.dtype)
        copy = pltpu.make_async_copy(held.at[:, at], grad.at[:, at], sems.at[k])
        copy.start()
        copies.append(copy)
    for copy in copies:
        copy.wait()


def last_part(gap_b, a, b, c, d, grad_in, sums_in, scale, weight):
    rows, width = a.shape
    spec = pl.BlockSpec(memory_space=pltpu.VMEM)
    return pl.pallas_call(
        functools.partial(last_kernel, scale, weight),
        in_specs=[spec] * 7,
        out_specs=[pl.BlockSpec(memory_space=pl.ANY), spec],
        out_shape=[jax.ShapeDtypeStruct((rows, width), jnp.bfloat16), jax.ShapeDtypeStruct((1, rows), jnp.float32)],
        scratch_shapes=[pltpu.VMEM((rows, width), jnp.bfloat16), pltpu.SemaphoreType.DMA((width // columns(width),))],
        cost_estimate=pl.CostEstimate(flops=8 * rows * rows * width, bytes_accessed=16 * rows * width, transcendentals=0),
        compiler_params=pltpu.CompilerParams(vmem_limit_bytes=VMEM_BYTES),
        name="last_part",
    )(gap_b, a, b, c, d, grad_in, sums_in)


def body(student, teacher):
    rows, width = student.shape
    window = (2 * REACH + 1) * rows
    scale = 1.0 / math.sqrt(width)
    index = lax.axis_index(AXIS)
    inner = (1 - ((index % 2) ^ ((index // 2) % 2))).astype(jnp.float32)
    lane = lax.broadcasted_iota(jnp.int32, (1, 4 * rows), 1)
    factors = jnp.where((lane >= rows) & (lane < 2 * rows), scale * inner, scale)

    s_side = move(student, partner)
    s_far = move(student, heavy)
    s_back = move(student, light)
    s_mate = move(student, swap)
    t_mate = move(teacher, swap)
    t_side = move(after(teacher, s_side), partner)
    t_far = move(after(teacher, s_far), heavy)
    s_diag = move(after(s_side, s_back), light)

    grad, sums = own_part(student, teacher, s_mate, t_mate, scale)
    s_side_mate = move(after(s_side, sums), swap)
    mine, out = student_grams(student, s_mate, s_side, s_side_mate, s_far)

    t_side_mate = move(after(t_side, out, t_far), swap)
    direct, cross = send_direct(t_far, teacher, t_mate, out, factors)
    out_gap = send_diag(t_far, t_side, t_side_mate, out, after(direct, s_diag), scale)
    cross_mate = move(cross, swap)
    s_diag_mate = move(after(s_diag, out_gap), swap)
    s_back_mate = move(after(s_back, out_gap), swap)
    s_far_mate = move(after(s_far, out_gap), swap)
    in_gap = move(out_gap, light)
    grad, sums = near_part(
        teacher, t_side, t_side_mate, t_far, mine, cross_mate,
        s_side, s_side_mate, s_far, s_far_mate, grad, sums, scale,
    )
    grad, sums = last_part(in_gap, s_back, s_back_mate, s_diag, s_diag_mate, grad, sums, 1.0 / math.sqrt(window), 1.0 / window)
    return grad, sums.reshape(rows)


def solution(mesh):
    return jax.shard_map(
        body,
        mesh=mesh,
        in_specs=(P(("parts", "blk"), None), P(("parts", "blk"), None)),
        out_specs=(P(("parts", "blk"), None), P(("parts", "blk"))),
        check_vma=False,
    )
```

```python
import functools
import math

import jax
import jax.numpy as jnp
from jax import lax
from jax.experimental import pallas as pl
from jax.experimental.pallas import tpu as pltpu
from jax.sharding import PartitionSpec as P

REACH = 4
AXIS = "blk"
LANES = 128
VMEM_BYTES = 9 * 1024 * 1024


def move(block, target):
    devices = range(lax.axis_size(AXIS))
    route = [(i, target(i)) for i in devices if target(i) is not None and target(i) in devices]
    return lax.ppermute(block, AXIS, route)


def odd_chip(i):
    return (i // 2) % 2


def partner(i):
    return i ^ 2


def heavy(i):
    return i + 4 if odd_chip(i) else i - 4


def light(i):
    return i - 4 if odd_chip(i) else i + 4


def swap(i):
    return i ^ 1


def after(block, *others):
    return lax.optimization_barrier((block, *others))[0]


def gram(a, b):
    return lax.dot_general(a, b, (((1,), (1,)), ((), ())), preferred_element_type=jnp.float32)


def lane_sums(x):
    total = x[:, :LANES]
    for k in range(1, x.shape[1] // LANES):
        total = total + x[:, k * LANES : (k + 1) * LANES]
    return total


def columns(width):
    for tile in (512, 384, 256, 128):
        if width % tile == 0:
            return tile
    return width


def call(kernel, ins, outs, scratch, flops, name, alias=None, streamed=()):
    nbytes = sum(x.size * x.dtype.itemsize for x in ins) + sum(math.prod(o.shape) * o.dtype.itemsize for o in outs)
    spec = pl.BlockSpec(memory_space=pltpu.VMEM)
    far = pl.BlockSpec(memory_space=pltpu.HBM)
    return pl.pallas_call(
        kernel,
        in_specs=[far if j in streamed else spec for j in range(len(ins))],
        out_specs=[spec] * len(outs),
        out_shape=outs,
        scratch_shapes=scratch,
        cost_estimate=pl.CostEstimate(flops=int(flops), bytes_accessed=int(nbytes), transcendentals=0),
        compiler_params=pltpu.CompilerParams(vmem_limit_bytes=VMEM_BYTES),
        input_output_aliases=alias or {},
        name=name,
    )(*ins)


def fetch(source, target, sems, tile):
    copies = []
    for k in range(source.shape[1] // tile):
        at = slice(k * tile, (k + 1) * tile)
        copies.append(pltpu.make_async_copy(source.at[:, at], target.at[:, at], sems.at[k]))
        copies[-1].start()
    return copies


def grams(rows_of, others, store):
    rows = rows_of.shape[0]
    for j, other in enumerate(others):
        store(slice(j * rows, (j + 1) * rows), gram(rows_of[...], other[...]))


def weigh(gap_b, others, put):
    width = others[0].shape[1]
    tile = columns(width)
    for k in range(width // tile):
        at = slice(k * tile, (k + 1) * tile)
        stack = jnp.concatenate([other[:, at] for other in others], axis=0)
        put(at, jnp.dot(gap_b[...], stack, preferred_element_type=jnp.float32))


def own_kernel(scale, s, t, s_mate, t_mate, grad, sums, gap_b):
    rows = s.shape[0]
    for j, (os, ot) in enumerate(((s, t), (s_mate, t_mate))):
        g = (gram(s[...], os[...]) - gram(t[...], ot[...])) * scale
        gap_b[:, j * rows : (j + 1) * rows] = g.astype(jnp.bfloat16)
    wide = gap_b[...].astype(jnp.float32)
    sums[...] = lane_sums(wide * wide)

    def put(at, value):
        grad[:, at] = value

    weigh(gap_b, (s, s_mate), put)


def own_part(s, t, s_mate, t_mate, scale):
    rows, width = s.shape
    return call(
        functools.partial(own_kernel, scale),
        (s, t, s_mate, t_mate),
        [jax.ShapeDtypeStruct((rows, width), jnp.float32), jax.ShapeDtypeStruct((rows, LANES), jnp.float32)],
        [pltpu.VMEM((rows, 2 * rows), jnp.bfloat16)],
        12 * rows * rows * width,
        "own_part",
    )


def student_grams_kernel(s, s_mate, x, f, mine, out):
    def store_mine(at, value):
        mine[:, at] = value

    def store_out(at, value):
        out[:, at] = value

    grams(s, (x, f), store_mine)
    grams(f, (s, s_mate, x), store_out)


def student_grams(*blocks):
    rows, width = blocks[0].shape
    shapes = [jax.ShapeDtypeStruct((rows, n * rows), jnp.float32) for n in (2, 3)]
    return call(student_grams_kernel, blocks, shapes, [], 10 * rows * rows * width, "student_grams")


def stage_kernel(*refs):
    *blocks, out, sems = refs
    rows = blocks[0].shape[0]
    copies = [
        pltpu.make_async_copy(block, out.at[j * rows : (j + 1) * rows], sems.at[j]) for j, block in enumerate(blocks)
    ]
    for copy in copies:
        copy.start()
    for copy in copies:
        copy.wait()


def stage(*blocks):
    rows, width = blocks[0].shape
    count = len(blocks)
    return call(
        stage_kernel, blocks, [jax.ShapeDtypeStruct((count * rows, width), jnp.bfloat16)],
        [pltpu.SemaphoreType.DMA((count,))], 0, "stage", streamed=tuple(range(count)),
    )[0]


def send_direct_kernel(f, three, student, factors, out, cross):
    rows = f.shape[0]
    g = ((student[...] - gram(f[...], three[...])) * factors[...]).astype(jnp.bfloat16)
    out[:, : 3 * rows] = g
    cross[...] = g[:, rows : 2 * rows]


def send_direct(f, three, student, factors):
    rows, width = f.shape
    return call(
        send_direct_kernel,
        (f, three, student, factors),
        [jax.ShapeDtypeStruct((rows, 4 * rows), jnp.bfloat16), jax.ShapeDtypeStruct((rows, rows), jnp.bfloat16)],
        [],
        6 * rows * rows * width,
        "send_direct",
    )


def send_diag_kernel(scale, f, tf, x_mate, tx_mate, direct, out):
    rows = f.shape[0]
    out[:, : 3 * rows] = direct[:, : 3 * rows]
    g = gram(f[...], x_mate[...]) - gram(tf[...], tx_mate[...])
    out[:, 3 * rows :] = (g * scale).astype(jnp.bfloat16)


def send_diag(f, tf, x_mate, tx_mate, direct, scale):
    rows, width = f.shape
    return call(
        functools.partial(send_diag_kernel, scale),
        (f, tf, x_mate, tx_mate, direct),
        [jax.ShapeDtypeStruct((rows, 4 * rows), jnp.bfloat16)],
        [],
        4 * rows * rows * width,
        "send_diag",
    )[0]


def near_kernel(
    scale, s, three, tx_mate, tf, student, cross, sx, sx_mate, sf, sf_mate, grad_in, sums_in, far,
    grad, sums, near, gap_b, sem
):
    rows = s.shape[0]
    copy = pltpu.make_async_copy(far, near, sem)
    copy.start()
    t, tx = three.at[:rows], three.at[2 * rows :]
    blocks = (
        student[:, :rows] - gram(t[...], tx[...]),
        gram(s[...], sx_mate[...]) - gram(t[...], tx_mate[...]),
        student[:, rows:] - gram(t[...], tf[...]),
    )
    for j, block in enumerate(blocks):
        gap_b[:, j * rows : (j + 1) * rows] = (block * scale).astype(jnp.bfloat16)
    gap_b[:, 3 * rows :] = cross[...].astype(jnp.float32).T.astype(jnp.bfloat16)
    wide = gap_b[...].astype(jnp.float32)
    sums[...] = sums_in[...] + lane_sums(wide * wide)

    def put(at, value):
        grad[:, at] = grad_in[:, at] + value

    weigh(gap_b, (sx, sx_mate, sf, sf_mate), put)
    copy.wait()


def near_part(s, three, tx_mate, tf, student, cross, sx, sx_mate, sf, sf_mate, grad_in, sums_in, far, scale):
    rows, width = s.shape
    return call(
        functools.partial(near_kernel, scale),
        (s, three, tx_mate, tf, student, cross, sx, sx_mate, sf, sf_mate, grad_in, sums_in, far),
        [
            jax.ShapeDtypeStruct((rows, width), jnp.float32),
            jax.ShapeDtypeStruct((rows, LANES), jnp.float32),
            jax.ShapeDtypeStruct((rows, width), jnp.bfloat16),
        ],
        [pltpu.VMEM((rows, 4 * rows), jnp.bfloat16), pltpu.SemaphoreType.DMA],
        16 * rows * rows * width,
        "near_part",
        {10: 0, 11: 1},
        streamed=(12,),
    )


def last_kernel(scale, weight, gap_b, a, b, c, d, grad_in, sums_in, grad, sums):
    def put(at, value):
        grad[:, at] = ((grad_in[:, at] + value) * scale).astype(grad.dtype)

    weigh(gap_b, (a, b, c, d), put)
    wide = gap_b[...].astype(jnp.float32)
    total = sums_in[...] + lane_sums(wide * wide)
    sums[...] = jnp.sum(total.T, axis=0, keepdims=True) * weight


def last_part(gap_b, a, b, c, d, grad_in, sums_in, scale, weight):
    rows, width = a.shape
    return call(
        functools.partial(last_kernel, scale, weight),
        (gap_b, a, b, c, d, grad_in, sums_in),
        [jax.ShapeDtypeStruct((rows, width), jnp.bfloat16), jax.ShapeDtypeStruct((1, rows), jnp.float32)],
        [],
        8 * rows * rows * width,
        "last_part",
    )


def body(student, teacher):
    rows, width = student.shape
    window = (2 * REACH + 1) * rows
    scale = 1.0 / math.sqrt(width)
    index = lax.axis_index(AXIS)
    inner = (1 - ((index % 2) ^ ((index // 2) % 2))).astype(jnp.float32)
    lane = lax.broadcasted_iota(jnp.int32, (1, 3 * rows), 1)
    factors = jnp.where((lane >= rows) & (lane < 2 * rows), scale * inner, scale)

    s_side = move(student, partner)
    s_far = move(student, heavy)
    s_back = move(student, light)
    s_mate = move(student, swap)
    t_mate = move(teacher, swap)
    grad, sums = own_part(student, teacher, s_mate, t_mate, scale)
    t_next = after(teacher, sums)
    t_side = move(t_next, partner)
    t_far = move(t_next, heavy)
    s_diag = move(after(s_side, s_back), light)
    mine, out = student_grams(student, s_mate, s_side, s_far)

    s_side_mate = move(after(s_side, out, t_side), swap)
    t_side_mate = move(after(t_side, out), swap)
    three = stage(teacher, t_mate, t_side)
    direct, cross = send_direct(t_far, three, out, factors)
    cross_mate = move(cross, swap)
    out_gap = send_diag(s_far, t_far, s_side_mate, t_side_mate, after(direct, cross_mate, s_diag), scale)
    s_far_mate = move(after(s_far, out_gap), swap)
    s_diag_mate = move(after(s_diag, out_gap), swap)
    s_back_mate = move(after(s_back, out_gap), swap)
    in_gap = move(out_gap, light)
    grad, sums, s_diag = near_part(
        student, three, t_side_mate, t_far, mine, cross_mate, s_side, s_side_mate, s_far, s_far_mate, grad, sums,
        s_diag, scale,
    )
    grad, sums = last_part(in_gap, s_back, s_back_mate, s_diag, s_diag_mate, grad, sums, 1.0 / math.sqrt(window), 1.0 / window)
    return grad, sums.reshape(rows)


def solution(mesh):
    return jax.shard_map(
        body,
        mesh=mesh,
        in_specs=(P(("parts", "blk"), None), P(("parts", "blk"), None)),
        out_specs=(P(("parts", "blk"), None), P(("parts", "blk"))),
        check_vma=False,
    )
```

```python
import functools
import math

import jax
import jax.numpy as jnp
from jax import lax
from jax.experimental import pallas as pl
from jax.experimental.pallas import tpu as pltpu
from jax.sharding import PartitionSpec as P

REACH = 4
AXIS = "blk"
LANES = 128
VMEM_BYTES = 9 * 1024 * 1024


def move(block, target):
    devices = range(lax.axis_size(AXIS))
    route = [(i, target(i)) for i in devices if target(i) is not None and target(i) in devices]
    return lax.ppermute(block, AXIS, route)


def odd_chip(i):
    return (i // 2) % 2


def partner(i):
    return i ^ 2


def heavy(i):
    return i + 4 if odd_chip(i) else i - 4


def light(i):
    return i - 4 if odd_chip(i) else i + 4


def swap(i):
    return i ^ 1


def after(block, *others):
    return lax.optimization_barrier((block, *others))[0]


def gram(a, b):
    return lax.dot_general(a, b, (((1,), (1,)), ((), ())), preferred_element_type=jnp.float32)


def lane_sums(x):
    total = x[:, :LANES]
    for k in range(1, x.shape[1] // LANES):
        total = total + x[:, k * LANES : (k + 1) * LANES]
    return total


def columns(width):
    for tile in (512, 384, 256, 128):
        if width % tile == 0:
            return tile
    return width


def call(kernel, ins, outs, scratch, flops, name, alias=None, streamed=(), free=False):
    nbytes = sum(x.size * x.dtype.itemsize for x in ins) + sum(math.prod(o.shape) * o.dtype.itemsize for o in outs)
    spec = pl.BlockSpec(memory_space=pltpu.VMEM)
    far = pl.BlockSpec(memory_space=pltpu.HBM)
    return pl.pallas_call(
        kernel,
        in_specs=[far if j in streamed else spec for j in range(len(ins))],
        out_specs=[spec] * len(outs),
        out_shape=outs,
        scratch_shapes=scratch,
        cost_estimate=pl.CostEstimate(flops=int(flops), bytes_accessed=0 if free else int(nbytes), transcendentals=0),
        compiler_params=pltpu.CompilerParams(vmem_limit_bytes=VMEM_BYTES),
        input_output_aliases=alias or {},
        name=name,
    )(*ins)


def fetch(source, target, sems, tile):
    copies = []
    for k in range(source.shape[1] // tile):
        at = slice(k * tile, (k + 1) * tile)
        copies.append(pltpu.make_async_copy(source.at[:, at], target.at[:, at], sems.at[k]))
        copies[-1].start()
    return copies


def grams(rows_of, others, store):
    rows = rows_of.shape[0]
    for j, other in enumerate(others):
        store(slice(j * rows, (j + 1) * rows), gram(rows_of[...], other[...]))


def weigh(gap_b, others, put):
    width = others[0].shape[1]
    tile = columns(width)
    for k in range(width // tile):
        at = slice(k * tile, (k + 1) * tile)
        stack = jnp.concatenate([other[:, at] for other in others], axis=0)
        put(at, jnp.dot(gap_b[...], stack, preferred_element_type=jnp.float32))


def own_kernel(scale, s, t, s_mate, t_mate, grad, sums, gap_b):
    rows = s.shape[0]
    for j, (os, ot) in enumerate(((s, t), (s_mate, t_mate))):
        g = (gram(s[...], os[...]) - gram(t[...], ot[...])) * scale
        gap_b[:, j * rows : (j + 1) * rows] = g.astype(jnp.bfloat16)
    wide = gap_b[...].astype(jnp.float32)
    sums[...] = lane_sums(wide * wide)

    def put(at, value):
        grad[:, at] = value

    weigh(gap_b, (s, s_mate), put)


def own_part(s, t, s_mate, t_mate, scale):
    rows, width = s.shape
    return call(
        functools.partial(own_kernel, scale),
        (s, t, s_mate, t_mate),
        [jax.ShapeDtypeStruct((rows, width), jnp.float32), jax.ShapeDtypeStruct((rows, LANES), jnp.float32)],
        [pltpu.VMEM((rows, 2 * rows), jnp.bfloat16)],
        12 * rows * rows * width,
        "own_part",
    )


def student_grams_kernel(s, s_mate, x, f, mine, out):
    def store_mine(at, value):
        mine[:, at] = value

    def store_out(at, value):
        out[:, at] = value

    grams(s, (x, f), store_mine)
    grams(f, (s, s_mate, x), store_out)


def student_grams(*blocks):
    rows, width = blocks[0].shape
    shapes = [jax.ShapeDtypeStruct((rows, n * rows), jnp.float32) for n in (2, 3)]
    return call(student_grams_kernel, blocks, shapes, [], 10 * rows * rows * width, "student_grams")


def stage_kernel(*refs):
    *blocks, out, sems = refs
    rows = blocks[0].shape[0]
    copies = [
        pltpu.make_async_copy(block, out.at[j * rows : (j + 1) * rows], sems.at[j]) for j, block in enumerate(blocks)
    ]
    for copy in copies:
        copy.start()
    for copy in copies:
        copy.wait()


def stage(*blocks):
    rows, width = blocks[0].shape
    count = len(blocks)
    return call(
        stage_kernel, blocks, [jax.ShapeDtypeStruct((count * rows, width), jnp.bfloat16)],
        [pltpu.SemaphoreType.DMA((count,))], 0, "stage", streamed=tuple(range(count)), free=True,
    )[0]


def send_direct_kernel(f, three, student, factors, out, cross):
    rows = f.shape[0]
    g = ((student[...] - gram(f[...], three[...])) * factors[...]).astype(jnp.bfloat16)
    out[:, : 3 * rows] = g
    cross[...] = g[:, rows : 2 * rows]


def send_direct(f, three, student, factors):
    rows, width = f.shape
    return call(
        send_direct_kernel,
        (f, three, student, factors),
        [jax.ShapeDtypeStruct((rows, 4 * rows), jnp.bfloat16), jax.ShapeDtypeStruct((rows, rows), jnp.bfloat16)],
        [],
        6 * rows * rows * width,
        "send_direct",
    )


def send_diag_kernel(scale, direct, mates, f, tf, out):
    rows = f.shape[0]
    x_mate, tx_mate = mates.at[:rows], mates.at[rows:]
    out[:, : 3 * rows] = direct[:, : 3 * rows]
    g = gram(f[...], x_mate[...]) - gram(tf[...], tx_mate[...])
    out[:, 3 * rows :] = (g * scale).astype(jnp.bfloat16)


def send_diag(direct, mates, f, tf, scale):
    rows, width = f.shape
    return call(
        functools.partial(send_diag_kernel, scale),
        (direct, mates, f, tf),
        [jax.ShapeDtypeStruct((rows, 4 * rows), jnp.bfloat16)],
        [],
        4 * rows * rows * width,
        "send_diag",
    )[0]


def near_kernel(
    scale, s, three, mates, tf, student, cross, sx, sf, sf_mate, grad_in, sums_in, far,
    grad, sums, near, gap_b, sem
):
    rows = s.shape[0]
    copy = pltpu.make_async_copy(far, near, sem)
    copy.start()
    t, tx = three.at[:rows], three.at[2 * rows :]
    sx_mate, tx_mate = mates.at[:rows], mates.at[rows:]
    blocks = (
        student[:, :rows] - gram(t[...], tx[...]),
        gram(s[...], sx_mate[...]) - gram(t[...], tx_mate[...]),
        student[:, rows:] - gram(t[...], tf[...]),
    )
    for j, block in enumerate(blocks):
        gap_b[:, j * rows : (j + 1) * rows] = (block * scale).astype(jnp.bfloat16)
    gap_b[:, 3 * rows :] = cross[...].astype(jnp.float32).T.astype(jnp.bfloat16)
    wide = gap_b[...].astype(jnp.float32)
    sums[...] = sums_in[...] + lane_sums(wide * wide)

    def put(at, value):
        grad[:, at] = grad_in[:, at] + value

    weigh(gap_b, (sx, sx_mate, sf, sf_mate), put)
    copy.wait()


def near_part(s, three, mates, tf, student, cross, sx, sf, sf_mate, grad_in, sums_in, far, scale):
    rows, width = s.shape
    return call(
        functools.partial(near_kernel, scale),
        (s, three, mates, tf, student, cross, sx, sf, sf_mate, grad_in, sums_in, far),
        [
            jax.ShapeDtypeStruct((rows, width), jnp.float32),
            jax.ShapeDtypeStruct((rows, LANES), jnp.float32),
            jax.ShapeDtypeStruct((rows, width), jnp.bfloat16),
        ],
        [pltpu.VMEM((rows, 4 * rows), jnp.bfloat16), pltpu.SemaphoreType.DMA],
        16 * rows * rows * width,
        "near_part",
        {9: 0, 10: 1},
        streamed=(11,),
    )


def last_kernel(scale, weight, gap_b, a, b, c, d, grad_in, sums_in, grad, sums):
    def put(at, value):
        grad[:, at] = ((grad_in[:, at] + value) * scale).astype(grad.dtype)

    weigh(gap_b, (a, b, c, d), put)
    wide = gap_b[...].astype(jnp.float32)
    total = sums_in[...] + lane_sums(wide * wide)
    sums[...] = jnp.sum(total.T, axis=0, keepdims=True) * weight


def last_part(gap_b, a, b, c, d, grad_in, sums_in, scale, weight):
    rows, width = a.shape
    return call(
        functools.partial(last_kernel, scale, weight),
        (gap_b, a, b, c, d, grad_in, sums_in),
        [jax.ShapeDtypeStruct((rows, width), jnp.bfloat16), jax.ShapeDtypeStruct((1, rows), jnp.float32)],
        [],
        8 * rows * rows * width,
        "last_part",
    )


def body(student, teacher):
    rows, width = student.shape
    window = (2 * REACH + 1) * rows
    scale = 1.0 / math.sqrt(width)
    index = lax.axis_index(AXIS)
    inner = (1 - ((index % 2) ^ ((index // 2) % 2))).astype(jnp.float32)
    lane = lax.broadcasted_iota(jnp.int32, (1, 3 * rows), 1)
    factors = jnp.where((lane >= rows) & (lane < 2 * rows), scale * inner, scale)

    s_side = move(student, partner)
    s_far = move(student, heavy)
    s_back = move(student, light)
    s_mate = move(student, swap)
    t_mate = move(teacher, swap)
    grad, sums = own_part(student, teacher, s_mate, t_mate, scale)
    t_next = after(teacher, sums)
    t_side = move(t_next, partner)
    t_far = move(t_next, heavy)
    s_diag = move(after(s_side, s_back), light)
    mine, out = student_grams(student, s_mate, s_side, s_far)

    s_side_mate = move(after(s_side, out, t_side), swap)
    t_side_mate = move(after(t_side, out), swap)
    three = stage(teacher, t_mate, t_side)
    direct, cross = send_direct(t_far, three, out, factors)
    cross_mate = move(cross, swap)
    mates = stage(s_side_mate, t_side_mate)
    _, direct, cross_mate = lax.optimization_barrier((s_diag, direct, cross_mate))
    out_gap = send_diag(direct, mates, s_far, t_far, scale)
    s_far_mate = move(after(s_far, out_gap), swap)
    s_diag_mate = move(after(s_diag, out_gap), swap)
    s_back_mate = move(after(s_back, out_gap), swap)
    in_gap = move(out_gap, light)
    grad, sums, s_diag = near_part(
        student, three, mates, t_far, mine, cross_mate, s_side, s_far, s_far_mate, grad, sums,
        s_diag, scale,
    )
    grad, sums = last_part(in_gap, s_back, s_back_mate, s_diag, s_diag_mate, grad, sums, 1.0 / math.sqrt(window), 1.0 / window)
    return grad, sums.reshape(rows)


def solution(mesh):
    return jax.shard_map(
        body,
        mesh=mesh,
        in_specs=(P(("parts", "blk"), None), P(("parts", "blk"), None)),
        out_specs=(P(("parts", "blk"), None), P(("parts", "blk"))),
        check_vma=False,
    )
```

```python
import functools
import math

import jax
import jax.numpy as jnp
from jax import lax
from jax.experimental import pallas as pl
from jax.experimental.pallas import tpu as pltpu
from jax.sharding import PartitionSpec as P

REACH = 4
AXIS = "blk"
LANES = 128
VMEM_BYTES = 9 * 1024 * 1024


def move(block, target):
    devices = range(lax.axis_size(AXIS))
    route = [(i, target(i)) for i in devices if target(i) is not None and target(i) in devices]
    return lax.ppermute(block, AXIS, route)


def odd_chip(i):
    return (i // 2) % 2


def partner(i):
    return i ^ 2


def heavy(i):
    return i + 4 if odd_chip(i) else i - 4


def light(i):
    return i - 4 if odd_chip(i) else i + 4


def swap(i):
    return i ^ 1


def after(block, *others):
    return lax.optimization_barrier((block, *others))[0]


def gram(a, b):
    return lax.dot_general(a, b, (((1,), (1,)), ((), ())), preferred_element_type=jnp.float32)


def lane_sums(x):
    total = x[:, :LANES]
    for k in range(1, x.shape[1] // LANES):
        total = total + x[:, k * LANES : (k + 1) * LANES]
    return total


def columns(width):
    for tile in (512, 384, 256, 128):
        if width % tile == 0:
            return tile
    return width


def call(kernel, ins, outs, scratch, flops, name, alias=None, streamed=(), free=False):
    nbytes = sum(x.size * x.dtype.itemsize for x in ins) + sum(math.prod(o.shape) * o.dtype.itemsize for o in outs)
    spec = pl.BlockSpec(memory_space=pltpu.VMEM)
    far = pl.BlockSpec(memory_space=pltpu.HBM)
    return pl.pallas_call(
        kernel,
        in_specs=[far if j in streamed else spec for j in range(len(ins))],
        out_specs=[spec] * len(outs),
        out_shape=outs,
        scratch_shapes=scratch,
        cost_estimate=pl.CostEstimate(flops=int(flops), bytes_accessed=0 if free else int(nbytes), transcendentals=0),
        compiler_params=pltpu.CompilerParams(vmem_limit_bytes=VMEM_BYTES),
        input_output_aliases=alias or {},
        name=name,
    )(*ins)


def fetch(source, target, sems, tile):
    copies = []
    for k in range(source.shape[1] // tile):
        at = slice(k * tile, (k + 1) * tile)
        copies.append(pltpu.make_async_copy(source.at[:, at], target.at[:, at], sems.at[k]))
        copies[-1].start()
    return copies


def grams(rows_of, others, store):
    rows = rows_of.shape[0]
    for j, other in enumerate(others):
        store(slice(j * rows, (j + 1) * rows), gram(rows_of[...], other[...]))


def weigh(gap_b, others, put):
    width = others[0].shape[1]
    tile = columns(width)
    for k in range(width // tile):
        at = slice(k * tile, (k + 1) * tile)
        stack = jnp.concatenate([other[:, at] for other in others], axis=0)
        put(at, jnp.dot(gap_b[...], stack, preferred_element_type=jnp.float32))


def own_kernel(scale, s, t, s_mate, t_mate, grad, sums, gap_b):
    rows = s.shape[0]
    for j, (os, ot) in enumerate(((s, t), (s_mate, t_mate))):
        g = (gram(s[...], os[...]) - gram(t[...], ot[...])) * scale
        gap_b[:, j * rows : (j + 1) * rows] = g.astype(jnp.bfloat16)
    wide = gap_b[...].astype(jnp.float32)
    sums[...] = lane_sums(wide * wide)

    def put(at, value):
        grad[:, at] = value

    weigh(gap_b, (s, s_mate), put)


def own_part(s, t, s_mate, t_mate, scale):
    rows, width = s.shape
    return call(
        functools.partial(own_kernel, scale),
        (s, t, s_mate, t_mate),
        [jax.ShapeDtypeStruct((rows, width), jnp.float32), jax.ShapeDtypeStruct((rows, LANES), jnp.float32)],
        [pltpu.VMEM((rows, 2 * rows), jnp.bfloat16)],
        12 * rows * rows * width,
        "own_part",
    )


def student_grams_kernel(s, s_mate, x, f, mine, out):
    def store_mine(at, value):
        mine[:, at] = value

    def store_out(at, value):
        out[:, at] = value

    grams(s, (x, f), store_mine)
    grams(f, (s, s_mate, x), store_out)


def student_grams(*blocks):
    rows, width = blocks[0].shape
    shapes = [jax.ShapeDtypeStruct((rows, n * rows), jnp.float32) for n in (2, 3)]
    return call(student_grams_kernel, blocks, shapes, [], 10 * rows * rows * width, "student_grams")


def stage_kernel(*refs):
    *blocks, out, sems = refs
    rows = blocks[0].shape[0]
    copies = [
        pltpu.make_async_copy(block, out.at[j * rows : (j + 1) * rows], sems.at[j]) for j, block in enumerate(blocks)
    ]
    for copy in copies:
        copy.start()
    for copy in copies:
        copy.wait()


def stage(*blocks):
    rows, width = blocks[0].shape
    count = len(blocks)
    return call(
        stage_kernel, blocks, [jax.ShapeDtypeStruct((count * rows, width), jnp.bfloat16)],
        [pltpu.SemaphoreType.DMA((count,))], 0, "stage", streamed=tuple(range(count)), free=True,
    )[0]


def send_direct_kernel(f, three, student, factors, out, cross, near):
    rows = f.shape[0]
    near[...] = f[...]
    g = ((student[...] - gram(f[...], three[...])) * factors[...]).astype(jnp.bfloat16)
    out[:, : 3 * rows] = g
    cross[...] = g[:, rows : 2 * rows]


def send_direct(f, three, student, factors):
    rows, width = f.shape
    return call(
        send_direct_kernel,
        (f, three, student, factors),
        [jax.ShapeDtypeStruct((rows, n), jnp.bfloat16) for n in (4 * rows, rows, width)],
        [],
        6 * rows * rows * width,
        "send_direct",
    )


def send_diag_kernel(scale, direct, mates, tf, out):
    rows = tf.shape[0]
    x_mate, tx_mate, f = mates.at[:rows], mates.at[rows : 2 * rows], mates.at[2 * rows :]
    out[:, : 3 * rows] = direct[:, : 3 * rows]
    g = gram(f[...], x_mate[...]) - gram(tf[...], tx_mate[...])
    out[:, 3 * rows :] = (g * scale).astype(jnp.bfloat16)


def send_diag(direct, mates, tf, scale):
    rows, width = tf.shape
    return call(
        functools.partial(send_diag_kernel, scale),
        (direct, mates, tf),
        [jax.ShapeDtypeStruct((rows, 4 * rows), jnp.bfloat16)],
        [],
        4 * rows * rows * width,
        "send_diag",
    )[0]


def near_kernel(
    scale, s, three, mates, tf, student, cross, sx, sf_mate, grad_in, sums_in, far,
    grad, sums, near, gap_b, sem
):
    rows = s.shape[0]
    copy = pltpu.make_async_copy(far.at[:, : s.shape[1]], near, sem)
    copy.start()
    t, tx = three.at[:rows], three.at[2 * rows :]
    sx_mate, tx_mate, sf = mates.at[:rows], mates.at[rows : 2 * rows], mates.at[2 * rows :]
    blocks = (
        student[:, :rows] - gram(t[...], tx[...]),
        gram(s[...], sx_mate[...]) - gram(t[...], tx_mate[...]),
        student[:, rows:] - gram(t[...], tf[...]),
    )
    for j, block in enumerate(blocks):
        gap_b[:, j * rows : (j + 1) * rows] = (block * scale).astype(jnp.bfloat16)
    gap_b[:, 3 * rows :] = cross[...].astype(jnp.float32).T.astype(jnp.bfloat16)
    wide = gap_b[...].astype(jnp.float32)
    sums[...] = sums_in[...] + lane_sums(wide * wide)

    def put(at, value):
        grad[:, at] = grad_in[:, at] + value

    weigh(gap_b, (sx, sx_mate, sf, sf_mate), put)
    copy.wait()


def near_part(s, three, mates, tf, student, cross, sx, sf_mate, grad_in, sums_in, far, scale):
    rows, width = s.shape
    return call(
        functools.partial(near_kernel, scale),
        (s, three, mates, tf, student, cross, sx, sf_mate, grad_in, sums_in, far),
        [
            jax.ShapeDtypeStruct((rows, width), jnp.float32),
            jax.ShapeDtypeStruct((rows, LANES), jnp.float32),
            jax.ShapeDtypeStruct((rows, width), jnp.bfloat16),
        ],
        [pltpu.VMEM((rows, 4 * rows), jnp.bfloat16), pltpu.SemaphoreType.DMA],
        16 * rows * rows * width,
        "near_part",
        {8: 0, 9: 1},
        streamed=(10,),
    )


def last_kernel(scale, weight, gap_b, a, b, c, d, grad_in, sums_in, grad, sums):
    def put(at, value):
        grad[:, at] = ((grad_in[:, at] + value) * scale).astype(grad.dtype)

    weigh(gap_b, (a, b, c, d), put)
    wide = gap_b[...].astype(jnp.float32)
    total = sums_in[...] + lane_sums(wide * wide)
    sums[...] = jnp.sum(total.T, axis=0, keepdims=True) * weight


def last_part(gap_b, a, b, c, d, grad_in, sums_in, scale, weight):
    rows, width = a.shape
    return call(
        functools.partial(last_kernel, scale, weight),
        (gap_b, a, b, c, d, grad_in, sums_in),
        [jax.ShapeDtypeStruct((rows, width), jnp.bfloat16), jax.ShapeDtypeStruct((1, rows), jnp.float32)],
        [],
        8 * rows * rows * width,
        "last_part",
    )


def body(student, teacher):
    rows, width = student.shape
    window = (2 * REACH + 1) * rows
    scale = 1.0 / math.sqrt(width)
    index = lax.axis_index(AXIS)
    inner = (1 - ((index % 2) ^ ((index // 2) % 2))).astype(jnp.float32)
    lane = lax.broadcasted_iota(jnp.int32, (1, 3 * rows), 1)
    factors = jnp.where((lane >= rows) & (lane < 2 * rows), scale * inner, scale)

    s_side = move(student, partner)
    s_far = move(student, heavy)
    s_back = move(student, light)
    s_mate = move(student, swap)
    t_mate = move(teacher, swap)
    grad, sums = own_part(student, teacher, s_mate, t_mate, scale)
    t_next = after(teacher, sums)
    t_side = move(t_next, partner)
    t_far = move(t_next, heavy)
    s_diag = move(after(jnp.pad(s_side, ((0, 0), (0, LANES))), s_back), light)
    mine, out = student_grams(student, s_mate, s_side, s_far)

    s_side_mate = move(after(s_side, out, t_side), swap)
    t_side_mate = move(after(t_side, out), swap)
    three = stage(teacher, t_mate, t_side)
    direct, cross, t_far = send_direct(t_far, three, out, factors)
    cross_mate = move(cross, swap)
    mates = stage(s_side_mate, t_side_mate, s_far)
    _, mates, cross_mate = lax.optimization_barrier((s_diag, mates, cross_mate))
    out_gap = send_diag(direct, mates, t_far, scale)
    s_far_mate = move(after(s_far, out_gap), swap)
    s_diag_mate = move(after(s_diag, out_gap), swap)
    s_back_mate = move(after(s_back, out_gap), swap)
    in_gap = move(out_gap, light)
    grad, sums, s_diag = near_part(
        student, three, mates, t_far, mine, cross_mate, s_side, s_far_mate, grad, sums,
        s_diag, scale,
    )
    grad, sums = last_part(in_gap, s_back, s_back_mate, s_diag, s_diag_mate, grad, sums, 1.0 / math.sqrt(window), 1.0 / window)
    return grad, sums.reshape(rows)


def solution(mesh):
    return jax.shard_map(
        body,
        mesh=mesh,
        in_specs=(P(("parts", "blk"), None), P(("parts", "blk"), None)),
        out_specs=(P(("parts", "blk"), None), P(("parts", "blk"))),
        check_vma=False,
    )
```
